32 devices in a mesh: blk: 16 (over z, x, core), grp: 2 (over y).
Axes of the slice: x: 2, y: 2, z: 4, core: 2. Of those that a mesh axis runs over, the one named last changes fastest.
Arguments:
- raw: bfloat16 [32, 1024, 2400], P(None, ('blk', 'grp')), may hold values from -1200 to 1200
- partner: int32 [3, 16], replicated, may hold values from 0 to 15, as said below
Outputs:
- cross: bfloat16 [3, 256, 1024, 128], P(None, 'grp', 'blk')
The draws below stay inside these ranges and needn't reach their ends.
Inputs may be any that keep to these rules, and one draw needn't show every extreme that they name: Each row pairs off the 16 blocks: no block is its own partner, and the partner of a block's partner is the block itself. No two rows are equal.
All inputs are finite; a program needn't handle non-finite values.
Results may differ from the reference program's by a relative error of at most 0.0065.
Values may be sent and summed in bfloat16 or wider, within the bound.
A program may use at most 128 MiB of HBM per device.

```python
import math
import jax
import jax.numpy as jnp
from jax import lax

L = 2400
F = 256
SEG = 32
BCH = 64
ROUNDS = 3
CHANNELS = 1024
N_BLK = 16


def draw_raw(key, part):
    key_base = jax.random.fold_in(key, 11)
    key_chan = jax.random.fold_in(key, 12)
    key_seg = jax.random.fold_in(key, 13)
    chan_scale = jnp.exp(jax.random.uniform(key_chan, (1, CHANNELS, 1), jnp.float32) * math.log(10.0))
    seg_scale = jnp.exp(jax.random.uniform(key_seg, (SEG, 1, 1), jnp.float32) * math.log(10.0))
    base_noise = jnp.clip(jax.random.normal(key_base, (SEG, CHANNELS, L), jnp.float32), -6.0, 6.0)
    return (base_noise * chan_scale * seg_scale).astype(jnp.bfloat16)


def draw_partner(key, part):
    relabel = jax.random.permutation(jax.random.fold_in(key, 21), N_BLK).astype(jnp.int32)
    round_pick = jax.random.permutation(jax.random.fold_in(key, 22), N_BLK - 1)[:ROUNDS].astype(jnp.int32)
    modulus = N_BLK - 1
    slot_index = jnp.arange(N_BLK, dtype=jnp.int32)[None, :]
    round_col = round_pick[:, None]
    mirrored = jnp.mod(2 * round_col - slot_index, modulus)
    paired = jnp.where(slot_index == modulus, round_col, jnp.where(mirrored == slot_index, modulus, mirrored))
    return jnp.zeros((ROUNDS, N_BLK), jnp.int32).at[:, relabel].set(relabel[paired])


def setup_inputs(seed: int = 0) -> dict:
    arg_keys = jax.random.split(jax.random.key(seed), 3)
    raw = draw_raw(jax.random.fold_in(arg_keys[2], 71), 0)
    partner = draw_partner(jax.random.fold_in(arg_keys[2], 71), 0)
    return dict(raw=raw, partner=partner)


first_bin = 8
epsilon = 1e-06

def dft_table(length, num_bins):
    sample_idx = lax.broadcasted_iota(jnp.int32, (length, num_bins), 0)
    bin_index = lax.broadcasted_iota(jnp.int32, (length, num_bins), 1) + first_bin
    phase_angle = (sample_idx * bin_index % length).astype(jnp.float32) * (2.0 * math.pi / length)
    return jnp.concatenate([jnp.cos(phase_angle), -jnp.sin(phase_angle)], axis=1).astype(jnp.bfloat16)

def whiten(samples, num_bins):
    seg_count, chan_count, length = samples.shape
    spectrum = jnp.dot(samples.reshape(seg_count * chan_count, length), dft_table(length, num_bins), preferred_element_type=jnp.float32).reshape(seg_count, chan_count, 2 * num_bins)
    real_part = spectrum[:, :, :num_bins]
    imag_part = spectrum[:, :, num_bins:]
    bin_power = lax.optimization_barrier(jnp.mean(real_part * real_part + imag_part * imag_part, axis=0))
    factor = lax.rsqrt(bin_power + epsilon)
    joined = jnp.concatenate([real_part * factor, imag_part * factor], axis=0)
    return jnp.transpose(joined, (2, 1, 0)).astype(jnp.bfloat16)

def reference(raw, partner):

    def block_white(index):
        block = lax.dynamic_slice_in_dim(raw, index * BCH, BCH, 1)
        return whiten(block, F)
    white_all = lax.map(block_white, jnp.arange(N_BLK, dtype=jnp.int32))
    norm_scale = 1.0 / math.sqrt(SEG)

    def round_cross(row):

        def bin_cross(bin_index):
            mine = white_all[:, bin_index].astype(jnp.float32)
            other = mine[row]
            flipped = jnp.concatenate([mine[..., SEG:], -mine[..., :SEG]], axis=-1)
            real_sum = jnp.einsum('bis,bjs->bij', mine, other)
            imag_sum = jnp.einsum('bis,bjs->bij', flipped, other)
            joined = jnp.concatenate([real_sum, imag_sum], axis=-1) * norm_scale
            return joined.reshape(N_BLK * BCH, 2 * BCH).astype(jnp.bfloat16)
        return lax.map(bin_cross, jnp.arange(F, dtype=jnp.int32))
    return lax.map(round_cross, partner)
```

```python
import functools
import math

import jax
import jax.numpy as jnp
from jax import lax
from jax.experimental import pallas as pl
from jax.experimental.pallas import tpu as pltpu
from jax.sharding import PartitionSpec as P

F = 256
first_bin = 8
epsilon = 1e-06
GATHER_BYTES = 40 * 2**20


def dft_table(length, num_bins):
    sample_idx = lax.broadcasted_iota(jnp.int32, (length, num_bins), 0)
    bin_index = lax.broadcasted_iota(jnp.int32, (length, num_bins), 1) + first_bin
    phase_angle = (sample_idx * bin_index % length).astype(jnp.float32) * (2.0 * math.pi / length)
    return jnp.concatenate([jnp.cos(phase_angle), -jnp.sin(phase_angle)], axis=1).astype(
        jnp.bfloat16
    )


def whiten(samples, num_bins):
    seg_count, chan_count, length = samples.shape
    spectrum = jnp.dot(
        samples.reshape(seg_count * chan_count, length),
        dft_table(length, num_bins),
        preferred_element_type=jnp.float32,
    ).reshape(seg_count, chan_count, 2, num_bins)
    bin_power = jnp.mean(jnp.sum(spectrum * spectrum, axis=2), axis=0)
    factor = lax.rsqrt(bin_power + epsilon)
    return (spectrum * factor[None, :, None, :]).astype(jnp.bfloat16)


def cross_kernel(scale, rounds, picks_ref, mine_ref, *refs):
    out_ref = refs[rounds]
    bins, _, width = mine_ref.shape
    half = width // 2
    lane = lax.broadcasted_iota(jnp.int32, (half, width), 1)
    sign = jnp.where(lane < half, scale, -scale).astype(jnp.float32)
    for f in range(bins):
        mine = mine_ref[f]
        for r in range(rounds):
            full = lax.dot_general(
                mine, refs[r][0, f], (((0,), (0,)), ((), ())), preferred_element_type=jnp.float32
            )
            turned = pltpu.roll(full[half:], half, 1)
            out_ref[r, f] = (turned * scale + full[:half] * sign).astype(out_ref.dtype)


def cross(mine, gathered, picks, step):
    bins, seg_count, width = mine.shape
    rounds = picks.shape[0]
    half = width // 2
    other = [
        pl.BlockSpec(
            (1, step, seg_count, width), functools.partial(lambda r, i, p: (p[r], i, 0, 0), r)
        )
        for r in range(rounds)
    ]
    return pl.pallas_call(
        functools.partial(cross_kernel, 1.0 / math.sqrt(seg_count), rounds),
        grid_spec=pltpu.PrefetchScalarGridSpec(
            num_scalar_prefetch=1,
            grid=(bins // step,),
            in_specs=[pl.BlockSpec((step, seg_count, width), lambda i, p: (i, 0, 0))] + other,
            out_specs=pl.BlockSpec((rounds, step, half, width), lambda i, p: (0, i, 0, 0)),
        ),
        out_shape=jax.ShapeDtypeStruct((rounds, bins, half, width), jnp.bfloat16),
        compiler_params=pltpu.CompilerParams(vmem_limit_bytes=32 * 2**20),
    )(picks, mine, *[gathered] * rounds)


def per_device(num_blocks, num_grp, raw, partner):
    white = whiten(raw, F)
    seg_count, chan_count, _, _ = white.shape
    own = F // num_grp
    white = lax.all_to_all(white, "grp", split_axis=3, concat_axis=1, tiled=True)
    spectra = jnp.transpose(white, (3, 0, 2, 1)).reshape(
        own, seg_count, 2 * num_grp * chan_count
    )
    picks = lax.dynamic_index_in_dim(partner, lax.axis_index("blk"), 1, keepdims=False)
    chunks = 1
    while spectra.size * 2 * num_blocks // chunks > GATHER_BYTES:
        chunks *= 2

    def one(part):
        return cross(part, lax.all_gather(part, "blk"), picks, 16)

    if chunks == 1:
        return one(spectra)
    result = lax.map(one, spectra.reshape(chunks, own // chunks, seg_count, -1))
    rounds = partner.shape[0]
    return jnp.moveaxis(result, 0, 1).reshape(rounds, own, *result.shape[3:])


def solution(mesh):
    placed = (P(None, ("blk", "grp"), None), P())
    return jax.shard_map(
        functools.partial(per_device, mesh.shape["blk"], mesh.shape["grp"]),
        mesh=mesh,
        in_specs=placed,
        out_specs=P(None, "grp", "blk", None),
        check_vma=False,
    )
```

```python
import functools
import math

import jax
import jax.numpy as jnp
from jax import lax
from jax.experimental import pallas as pl
from jax.experimental.pallas import tpu as pltpu
from jax.sharding import PartitionSpec as P

F = 256
first_bin = 8
epsilon = 1e-06
GATHER_BYTES = 40 * 2**20


COARSE = 32


def dft_table(length, num_bins):
    bins = lax.broadcasted_iota(jnp.int32, (1, num_bins), 1) + first_bin
    unit = 2.0 * math.pi / length

    def pair(times):
        phase = (times[:, None] * bins % length).astype(jnp.float32) * unit
        return jnp.cos(phase), jnp.sin(phase)

    cos_a, sin_a = (t[:, None, :] for t in pair(jnp.arange(length // COARSE, dtype=jnp.int32) * COARSE))
    cos_b, sin_b = (t[None] for t in pair(jnp.arange(COARSE, dtype=jnp.int32)))
    table = jnp.concatenate(
        [cos_a * cos_b - sin_a * sin_b, -(sin_a * cos_b + cos_a * sin_b)], axis=2
    )
    return table.reshape(length, 2 * num_bins).astype(jnp.bfloat16)


def whiten(samples, num_bins):
    seg_count, chan_count, length = samples.shape
    spectrum = jnp.dot(
        samples.reshape(seg_count * chan_count, length),
        dft_table(length, num_bins),
        preferred_element_type=jnp.float32,
    ).reshape(seg_count, chan_count, 2 * num_bins)
    real_part = spectrum[:, :, :num_bins]
    imag_part = spectrum[:, :, num_bins:]
    bin_power = jnp.mean(real_part * real_part + imag_part * imag_part, axis=0)
    factor = lax.rsqrt(bin_power + epsilon)
    return jnp.stack([real_part * factor, imag_part * factor], axis=0).astype(jnp.bfloat16)


def cross_kernel(scale, rounds, picks_ref, mine_ref, *refs):
    out_ref = refs[rounds]
    bins, _, width = mine_ref.shape
    half = width // 2
    lane = lax.broadcasted_iota(jnp.int32, (half, width), 1)
    sign = jnp.where(lane < half, scale, -scale).astype(jnp.float32)
    for f in range(bins):
        mine = mine_ref[f]
        for r in range(rounds):
            full = lax.dot_general(
                mine, refs[r][0, f], (((0,), (0,)), ((), ())), preferred_element_type=jnp.float32
            )
            turned = pltpu.roll(full[half:], half, 1)
            out_ref[r, f] = (turned * scale + full[:half] * sign).astype(out_ref.dtype)


def cross(mine, gathered, picks, step):
    bins, seg_count, width = mine.shape
    rounds = picks.shape[0]
    half = width // 2
    other = [
        pl.BlockSpec(
            (1, step, seg_count, width), functools.partial(lambda r, i, p: (p[r], i, 0, 0), r)
        )
        for r in range(rounds)
    ]
    return pl.pallas_call(
        functools.partial(cross_kernel, 1.0 / math.sqrt(seg_count), rounds),
        grid_spec=pltpu.PrefetchScalarGridSpec(
            num_scalar_prefetch=1,
            grid=(bins // step,),
            in_specs=[pl.BlockSpec((step, seg_count, width), lambda i, p: (i, 0, 0))] + other,
            out_specs=pl.BlockSpec((rounds, step, half, width), lambda i, p: (0, i, 0, 0)),
        ),
        out_shape=jax.ShapeDtypeStruct((rounds, bins, half, width), jnp.bfloat16),
        compiler_params=pltpu.CompilerParams(vmem_limit_bytes=56 * 2**20),
    )(picks, mine, *[gathered] * rounds)


def gather_kernel(outer, cuts, x_ref, out_ref, z_sem, x_sem, c_sem, recv_sem):
    me = lax.axis_index("blk")
    o, m, c = me // 4, me // 2 % 2, me % 2
    pieces = len(cuts) - 1

    def index(o_, m_, c_):
        return (o_ * 2 + m_) * 2 + c_

    left, right = index(o - 1, m, c), index(o + 1, m, c)
    across, sibling = index(o, 1 - m, c), index(o, m, 1 - c)
    has_left, has_right = o > 0, o < outer - 1

    def copy(block, q, target, sem, own=False):
        part = pl.ds(cuts[q], cuts[q + 1] - cuts[q])
        there = out_ref.at[block, part]
        return pltpu.make_async_remote_copy(
            src_ref=x_ref.at[part] if own else there,
            dst_ref=there,
            send_sem=sem,
            recv_sem=recv_sem.at[block, q],
            device_id={"blk": target},
            device_id_type=pl.DeviceIdType.MESH,
        )

    def forward(act, o_, side, q, to_left, to_right, own=False):
        block = index(o_, m if side == 0 else 1 - m, c)
        if to_left:
            pl.when(has_left)(lambda: act(copy(block, q, left, z_sem.at[0, side, o_, q], own)))
        if to_right:
            pl.when(has_right)(lambda: act(copy(block, q, right, z_sem.at[1, side, o_, q], own)))
        if side == 0 and (own or q > 0):
            act(copy(block, q, across, x_sem.at[o_, q], own))
        act(copy(block, q, sibling, c_sem.at[side, o_, q], own))

    def sweep(act, arrive):
        for q in range(pieces):
            forward(act, o, 0, q, True, True, own=True)
        for step in range(1, outer + 1):
            for q in range(pieces):
                for side, far in ((0, step), (1, step - 1)):
                    line = side == 0 or q == 0
                    if far == 0:
                        arrive(o, side, q)
                        forward(act, o, side, q, line, line)
                    elif far < outer:

                        @pl.when(o - far >= 0)
                        def _():
                            arrive(o - far, side, q)
                            forward(act, o - far, side, q, False, line)

                        @pl.when(o + far < outer)
                        def _():
                            arrive(o + far, side, q)
                            forward(act, o + far, side, q, line, False)

    def arrive(o_, side, q):
        copy(index(o_, m if side == 0 else 1 - m, c), q, sibling, c_sem.at[0, 0, 0]).wait_recv()

    barrier = pltpu.get_barrier_semaphore()

    def greet(target):
        pl.semaphore_signal(
            barrier, inc=1, device_id={"blk": target}, device_id_type=pl.DeviceIdType.MESH
        )

    greet(across)
    greet(sibling)
    pl.when(has_left)(lambda: greet(left))
    pl.when(has_right)(lambda: greet(right))
    pl.semaphore_wait(barrier, 2 + jnp.minimum(o, 1) + jnp.minimum(outer - 1 - o, 1))

    sweep(lambda d: d.start(), arrive)
    for o_ in range(outer):
        for m_ in range(2):
            for q in range(pieces):
                copy(index(o_, m_, 1 - c), q, sibling, c_sem.at[0, 0, 0]).wait_recv()
    sweep(lambda d: d.wait_send(), lambda *_: None)


def gather(block, num_blocks):
    bins = block.shape[0]
    outer = num_blocks // 4
    cuts = tuple(bins * k // 16 for k in (0, 3, 7, 11, 16))
    pieces = len(cuts) - 1
    return pl.pallas_call(
        functools.partial(gather_kernel, outer, cuts),
        out_shape=jax.ShapeDtypeStruct((num_blocks, *block.shape), block.dtype),
        in_specs=[pl.BlockSpec(memory_space=pl.ANY)],
        out_specs=pl.BlockSpec(memory_space=pl.ANY),
        scratch_shapes=[
            pltpu.SemaphoreType.DMA((2, 2, outer, pieces)),
            pltpu.SemaphoreType.DMA((outer, pieces)),
            pltpu.SemaphoreType.DMA((2, outer, pieces)),
            pltpu.SemaphoreType.DMA((num_blocks, pieces)),
        ],
        compiler_params=pltpu.CompilerParams(
            collective_id=0, has_side_effects=True, vmem_limit_bytes=56 * 2**20
        ),
    )(block)


def per_device(num_blocks, num_grp, raw, partner):
    white = whiten(raw, F)
    _, seg_count, chan_count, _ = white.shape
    own = F // num_grp
    if num_grp == 2:
        me = lax.axis_index("grp")
        kept = lax.dynamic_slice_in_dim(white, me * own, own, 3)
        sent = lax.dynamic_slice_in_dim(white, (1 - me) * own, own, 3)
        got = lax.ppermute(sent, "grp", [(0, 1), (1, 0)])
        white = jnp.concatenate(
            [jnp.where(me == 0, kept, got), jnp.where(me == 0, got, kept)], axis=2
        )
    else:
        white = lax.all_to_all(white, "grp", split_axis=3, concat_axis=2, tiled=True)
    spectra = jnp.transpose(white, (3, 1, 0, 2)).reshape(
        own, seg_count, 2 * num_grp * chan_count
    )
    picks = lax.dynamic_index_in_dim(partner, lax.axis_index("blk"), 1, keepdims=False)
    chunks = 1
    while spectra.size * 2 * num_blocks // chunks > GATHER_BYTES:
        chunks *= 2

    direct = chunks == 1 and num_blocks % 4 == 0

    def one(part):
        whole = gather(part, num_blocks) if direct else lax.all_gather(part, "blk")
        return cross(part, whole, picks, 16)

    if chunks == 1:
        return one(spectra)
    result = lax.map(one, spectra.reshape(chunks, own // chunks, seg_count, -1))
    rounds = partner.shape[0]
    return jnp.moveaxis(result, 0, 1).reshape(rounds, own, *result.shape[3:])


def solution(mesh):
    placed = (P(None, ("blk", "grp"), None), P())
    return jax.shard_map(
        functools.partial(per_device, mesh.shape["blk"], mesh.shape["grp"]),
        mesh=mesh,
        in_specs=placed,
        out_specs=P(None, "grp", "blk", None),
        check_vma=False,
    )
```

```python
import functools
import math

import jax
import jax.numpy as jnp
from jax import lax
from jax.experimental import pallas as pl
from jax.experimental.pallas import tpu as pltpu
from jax.sharding import PartitionSpec as P

F = 256
first_bin = 8
epsilon = 1e-06
GATHER_BYTES = 40 * 2**20


COARSE = 32


def dft_table(length, first, num_bins):
    bins = lax.broadcasted_iota(jnp.int32, (1, num_bins), 1) + first
    unit = 2.0 * math.pi / length

    def pair(times):
        phase = (times[:, None] * bins % length).astype(jnp.float32) * unit
        return jnp.cos(phase), jnp.sin(phase)

    cos_a, sin_a = (t[:, None, :] for t in pair(jnp.arange(length // COARSE, dtype=jnp.int32) * COARSE))
    cos_b, sin_b = (t[None] for t in pair(jnp.arange(COARSE, dtype=jnp.int32)))
    table = jnp.concatenate(
        [cos_a * cos_b - sin_a * sin_b, -(sin_a * cos_b + cos_a * sin_b)], axis=2
    )
    return table.reshape(length, 2 * num_bins).astype(jnp.bfloat16)


def whiten(samples, first, num_bins):
    seg_count, chan_count, length = samples.shape
    spectrum = jnp.dot(
        samples.reshape(seg_count * chan_count, length),
        dft_table(length, first, num_bins),
        preferred_element_type=jnp.float32,
    ).reshape(seg_count, chan_count, 2 * num_bins)
    real_part = spectrum[:, :, :num_bins]
    imag_part = spectrum[:, :, num_bins:]
    bin_power = jnp.mean(real_part * real_part + imag_part * imag_part, axis=0)
    factor = lax.rsqrt(bin_power + epsilon)
    return jnp.stack([real_part * factor, imag_part * factor], axis=0).astype(jnp.bfloat16)


def cross_kernel(scale, rounds, picks_ref, mine_ref, *refs):
    out_ref = refs[rounds]
    bins, _, width = mine_ref.shape
    half = width // 2
    lane = lax.broadcasted_iota(jnp.int32, (half, width), 1)
    sign = jnp.where(lane < half, scale, -scale).astype(jnp.float32)
    for f in range(bins):
        mine = mine_ref[f]
        for r in range(rounds):
            full = lax.dot_general(
                mine, refs[r][0, f], (((0,), (0,)), ((), ())), preferred_element_type=jnp.float32
            )
            turned = pltpu.roll(full[half:], half, 1)
            out_ref[r, f] = (turned * scale + full[:half] * sign).astype(out_ref.dtype)


def cross(mine, gathered, picks, step):
    bins, seg_count, width = mine.shape
    rounds = picks.shape[0]
    half = width // 2
    other = [
        pl.BlockSpec(
            (1, step, seg_count, width), functools.partial(lambda r, i, p: (p[r], i, 0, 0), r)
        )
        for r in range(rounds)
    ]
    return pl.pallas_call(
        functools.partial(cross_kernel, 1.0 / math.sqrt(seg_count), rounds),
        grid_spec=pltpu.PrefetchScalarGridSpec(
            num_scalar_prefetch=1,
            grid=(bins // step,),
            in_specs=[pl.BlockSpec((step, seg_count, width), lambda i, p: (i, 0, 0))] + other,
            out_specs=pl.BlockSpec((rounds, step, half, width), lambda i, p: (0, i, 0, 0)),
        ),
        out_shape=jax.ShapeDtypeStruct((rounds, bins, half, width), jnp.bfloat16),
        compiler_params=pltpu.CompilerParams(vmem_limit_bytes=56 * 2**20),
    )(picks, mine, *[gathered] * rounds)


def gather_kernel(outer, cuts, x_ref, out_ref, z_sem, x_sem, c_sem, recv_sem):
    me = lax.axis_index("blk")
    o, m, c = me // 4, me // 2 % 2, me % 2
    pieces = len(cuts) - 1

    def index(o_, m_, c_):
        return (o_ * 2 + m_) * 2 + c_

    left, right = index(o - 1, m, c), index(o + 1, m, c)
    across, sibling = index(o, 1 - m, c), index(o, m, 1 - c)
    has_left, has_right = o > 0, o < outer - 1

    def copy(block, q, target, sem, own=False):
        part = pl.ds(cuts[q], cuts[q + 1] - cuts[q])
        there = out_ref.at[block, part]
        return pltpu.make_async_remote_copy(
            src_ref=x_ref.at[part] if own else there,
            dst_ref=there,
            send_sem=sem,
            recv_sem=recv_sem.at[block, q],
            device_id={"blk": target},
            device_id_type=pl.DeviceIdType.MESH,
        )

    def forward(act, o_, side, q, to_left, to_right, own=False):
        block = index(o_, m if side == 0 else 1 - m, c)
        if to_left:
            pl.when(has_left)(lambda: act(copy(block, q, left, z_sem.at[0, side, o_, q], own)))
        if to_right:
            pl.when(has_right)(lambda: act(copy(block, q, right, z_sem.at[1, side, o_, q], own)))
        if side == 0 and (own or q > 0):
            act(copy(block, q, across, x_sem.at[o_, q], own))
        act(copy(block, q, sibling, c_sem.at[side, o_, q], own))

    def sweep(act, arrive):
        for q in range(pieces):
            forward(act, o, 0, q, True, True, own=True)
        for step in range(1, outer + 1):
            for q in range(pieces):
                for side, far in ((0, step), (1, step - 1)):
                    line = side == 0 or q == 0
                    if far == 0:
                        arrive(o, side, q)
                        forward(act, o, side, q, line, line)
                    elif far < outer:

                        @pl.when(o - far >= 0)
                        def _():
                            arrive(o - far, side, q)
                            forward(act, o - far, side, q, False, line)

                        @pl.when(o + far < outer)
                        def _():
                            arrive(o + far, side, q)
                            forward(act, o + far, side, q, line, False)

    def arrive(o_, side, q):
        copy(index(o_, m if side == 0 else 1 - m, c), q, sibling, c_sem.at[0, 0, 0]).wait_recv()

    barrier = pltpu.get_barrier_semaphore()

    def greet(target):
        pl.semaphore_signal(
            barrier, inc=1, device_id={"blk": target}, device_id_type=pl.DeviceIdType.MESH
        )

    greet(across)
    greet(sibling)
    pl.when(has_left)(lambda: greet(left))
    pl.when(has_right)(lambda: greet(right))
    pl.semaphore_wait(barrier, 2 + jnp.minimum(o, 1) + jnp.minimum(outer - 1 - o, 1))

    sweep(lambda d: d.start(), arrive)
    for o_ in range(outer):
        for m_ in range(2):
            for q in range(pieces):
                copy(index(o_, m_, 1 - c), q, sibling, c_sem.at[0, 0, 0]).wait_recv()
    sweep(lambda d: d.wait_send(), lambda *_: None)


def gather(block, num_blocks):
    bins = block.shape[0]
    outer = num_blocks // 4
    cuts = tuple(bins * k // 16 for k in (0, 2, 7, 12, 16))
    pieces = len(cuts) - 1
    return pl.pallas_call(
        functools.partial(gather_kernel, outer, cuts),
        out_shape=jax.ShapeDtypeStruct((num_blocks, *block.shape), block.dtype),
        in_specs=[pl.BlockSpec(memory_space=pl.ANY)],
        out_specs=pl.BlockSpec(memory_space=pl.ANY),
        scratch_shapes=[
            pltpu.SemaphoreType.DMA((2, 2, outer, pieces)),
            pltpu.SemaphoreType.DMA((outer, pieces)),
            pltpu.SemaphoreType.DMA((2, outer, pieces)),
            pltpu.SemaphoreType.DMA((num_blocks, pieces)),
        ],
        compiler_params=pltpu.CompilerParams(
            collective_id=0, has_side_effects=True, vmem_limit_bytes=56 * 2**20
        ),
    )(block)


def per_device(num_blocks, num_grp, raw, partner):
    seg_count, chan_count, _ = raw.shape
    own = F // num_grp
    if num_grp == 2:
        me = lax.axis_index("grp")
        got = lax.ppermute(whiten(raw, first_bin + (1 - me) * own, own), "grp", [(0, 1), (1, 0)])
        kept = whiten(raw, first_bin + me * own, own)
        white = jnp.concatenate(
            [jnp.where(me == 0, kept, got), jnp.where(me == 0, got, kept)], axis=2
        )
    else:
        white = lax.all_to_all(whiten(raw, first_bin, F), "grp", split_axis=3, concat_axis=2, tiled=True)
    spectra = jnp.transpose(white, (3, 1, 0, 2)).reshape(
        own, seg_count, 2 * num_grp * chan_count
    )
    picks = lax.dynamic_index_in_dim(partner, lax.axis_index("blk"), 1, keepdims=False)
    chunks = 1
    while spectra.size * 2 * num_blocks // chunks > GATHER_BYTES:
        chunks *= 2

    direct = chunks == 1 and num_blocks % 4 == 0

    def one(part):
        whole = gather(part, num_blocks) if direct else lax.all_gather(part, "blk")
        return cross(part, whole, picks, 16)

    if chunks == 1:
        return one(spectra)
    result = lax.map(one, spectra.reshape(chunks, own // chunks, seg_count, -1))
    rounds = partner.shape[0]
    return jnp.moveaxis(result, 0, 1).reshape(rounds, own, *result.shape[3:])


def solution(mesh):
    placed = (P(None, ("blk", "grp"), None), P())
    return jax.shard_map(
        functools.partial(per_device, mesh.shape["blk"], mesh.shape["grp"]),
        mesh=mesh,
        in_specs=placed,
        out_specs=P(None, "grp", "blk", None),
        check_vma=False,
    )
```

```python
import functools
import math

import jax
import jax.numpy as jnp
from jax import lax
from jax.experimental import pallas as pl
from jax.experimental.pallas import tpu as pltpu
from jax.sharding import PartitionSpec as P

F = 256
first_bin = 8
epsilon = 1e-06
GATHER_BYTES = 40 * 2**20


COARSE = 32


def dft_table(length, first, num_bins):
    bins = lax.broadcasted_iota(jnp.int32, (1, num_bins), 1) + first
    unit = 2.0 * math.pi / length

    def pair(times):
        phase = (times[:, None] * bins % length).astype(jnp.float32) * unit
        return jnp.cos(phase), jnp.sin(phase)

    cos_a, sin_a = (t[:, None, :] for t in pair(jnp.arange(length // COARSE, dtype=jnp.int32) * COARSE))
    cos_b, sin_b = (t[None] for t in pair(jnp.arange(COARSE, dtype=jnp.int32)))
    table = jnp.concatenate(
        [cos_a * cos_b - sin_a * sin_b, -(sin_a * cos_b + cos_a * sin_b)], axis=2
    )
    return table.reshape(length, 2 * num_bins).astype(jnp.bfloat16)


def whiten(samples, first, num_bins):
    seg_count, chan_count, length = samples.shape
    spectrum = jnp.dot(
        samples.reshape(seg_count * chan_count, length),
        dft_table(length, first, num_bins),
        preferred_element_type=jnp.float32,
    ).reshape(seg_count, chan_count, 2 * num_bins)
    real_part = spectrum[:, :, :num_bins]
    imag_part = spectrum[:, :, num_bins:]
    bin_power = jnp.mean(real_part * real_part + imag_part * imag_part, axis=0)
    factor = lax.rsqrt(bin_power + epsilon)
    return jnp.stack([real_part * factor, imag_part * factor], axis=0).astype(jnp.bfloat16)


def cross_kernel(scale, rounds, picks_ref, mine_ref, *refs):
    out_ref = refs[rounds]
    bins, _, width = mine_ref.shape
    half = width // 2
    lane = lax.broadcasted_iota(jnp.int32, (half, width), 1)
    sign = jnp.where(lane < half, scale, -scale).astype(jnp.float32)
    for f in range(bins):
        mine = mine_ref[f]
        for r in range(rounds):
            full = lax.dot_general(
                mine, refs[r][0, f], (((0,), (0,)), ((), ())), preferred_element_type=jnp.float32
            )
            turned = pltpu.roll(full[half:], half, 1)
            out_ref[r, f] = (turned * scale + full[:half] * sign).astype(out_ref.dtype)


def cross(mine, gathered, picks, step):
    bins, seg_count, width = mine.shape
    rounds = picks.shape[0]
    half = width // 2
    other = [
        pl.BlockSpec(
            (1, step, seg_count, width), functools.partial(lambda r, i, p: (p[r], i, 0, 0), r)
        )
        for r in range(rounds)
    ]
    return pl.pallas_call(
        functools.partial(cross_kernel, 1.0 / math.sqrt(seg_count), rounds),
        grid_spec=pltpu.PrefetchScalarGridSpec(
            num_scalar_prefetch=1,
            grid=(bins // step,),
            in_specs=[pl.BlockSpec((step, seg_count, width), lambda i, p: (i, 0, 0))] + other,
            out_specs=pl.BlockSpec((rounds, step, half, width), lambda i, p: (0, i, 0, 0)),
        ),
        out_shape=jax.ShapeDtypeStruct((rounds, bins, half, width), jnp.bfloat16),
        compiler_params=pltpu.CompilerParams(vmem_limit_bytes=56 * 2**20),
    )(picks, mine, *[gathered] * rounds)


def gather_kernel(outer, cuts, x_ref, out_ref, z_sem, x_sem, c_sem, recv_sem):
    me = lax.axis_index("blk")
    o, m, c = me // 4, me // 2 % 2, me % 2
    pieces = len(cuts) - 1

    def index(o_, m_, c_):
        return (o_ * 2 + m_) * 2 + c_

    left, right = index(o - 1, m, c), index(o + 1, m, c)
    across, sibling = index(o, 1 - m, c), index(o, m, 1 - c)
    has_left, has_right = o > 0, o < outer - 1

    def copy(block, q, target, sem, own=False):
        part = pl.ds(cuts[q], cuts[q + 1] - cuts[q])
        there = out_ref.at[block, part]
        return pltpu.make_async_remote_copy(
            src_ref=x_ref.at[part] if own else there,
            dst_ref=there,
            send_sem=sem,
            recv_sem=recv_sem.at[block, q],
            device_id={"blk": target},
            device_id_type=pl.DeviceIdType.MESH,
        )

    def forward(act, o_, side, q, to_left, to_right, own=False):
        block = index(o_, m if side == 0 else 1 - m, c)
        if to_left:
            pl.when(has_left)(lambda: act(copy(block, q, left, z_sem.at[0, side, o_, q], own)))
        if to_right:
            pl.when(has_right)(lambda: act(copy(block, q, right, z_sem.at[1, side, o_, q], own)))
        if side == 0 and (own or q > 0):
            act(copy(block, q, across, x_sem.at[o_, q], own))
        act(copy(block, q, sibling, c_sem.at[side, o_, q], own))

    def sweep(act, arrive):
        for q in range(pieces):
            forward(act, o, 0, q, True, True, own=True)
        for step in range(1, outer + 1):
            for q in range(pieces):
                for side, far in ((0, step), (1, step - 1)):
                    line = side == 0 or q == 0
                    if far == 0:
                        arrive(o, side, q)
                        forward(act, o, side, q, line, line)
                    elif far < outer:

                        @pl.when(o - far >= 0)
                        def _():
                            arrive(o - far, side, q)
                            forward(act, o - far, side, q, False, line)

                        @pl.when(o + far < outer)
                        def _():
                            arrive(o + far, side, q)
                            forward(act, o + far, side, q, line, False)

    def arrive(o_, side, q):
        copy(index(o_, m if side == 0 else 1 - m, c), q, sibling, c_sem.at[0, 0, 0]).wait_recv()

    barrier = pltpu.get_barrier_semaphore()

    def greet(target):
        pl.semaphore_signal(
            barrier, inc=1, device_id={"blk": target}, device_id_type=pl.DeviceIdType.MESH
        )

    greet(across)
    greet(sibling)
    pl.when(has_left)(lambda: greet(left))
    pl.when(has_right)(lambda: greet(right))
    pl.semaphore_wait(barrier, 2 + jnp.minimum(o, 1) + jnp.minimum(outer - 1 - o, 1))

    sweep(lambda d: d.start(), arrive)
    for o_ in range(outer):
        for m_ in range(2):
            for q in range(pieces):
                copy(index(o_, m_, 1 - c), q, sibling, c_sem.at[0, 0, 0]).wait_recv()
    sweep(lambda d: d.wait_send(), lambda *_: None)


def gather(block, num_blocks):
    bins = block.shape[0]
    outer = num_blocks // 4
    cuts = tuple(bins * k // 16 for k in (0, 2, 5, 8, 11, 14, 16))
    pieces = len(cuts) - 1
    return pl.pallas_call(
        functools.partial(gather_kernel, outer, cuts),
        out_shape=jax.ShapeDtypeStruct((num_blocks, *block.shape), block.dtype),
        in_specs=[pl.BlockSpec(memory_space=pl.ANY)],
        out_specs=pl.BlockSpec(memory_space=pl.ANY),
        scratch_shapes=[
            pltpu.SemaphoreType.DMA((2, 2, outer, pieces)),
            pltpu.SemaphoreType.DMA((outer, pieces)),
            pltpu.SemaphoreType.DMA((2, outer, pieces)),
            pltpu.SemaphoreType.DMA((num_blocks, pieces)),
        ],
        compiler_params=pltpu.CompilerParams(
            collective_id=0, has_side_effects=True, vmem_limit_bytes=56 * 2**20
        ),
    )(block)


def per_device(num_blocks, num_grp, raw, partner):
    seg_count, chan_count, _ = raw.shape
    own = F // num_grp
    if num_grp == 2:
        me = lax.axis_index("grp")
        got = lax.ppermute(whiten(raw, first_bin + (1 - me) * own, own), "grp", [(0, 1), (1, 0)])
        kept = whiten(raw, first_bin + me * own, own)
        white = jnp.concatenate(
            [jnp.where(me == 0, kept, got), jnp.where(me == 0, got, kept)], axis=2
        )
    else:
        white = lax.all_to_all(whiten(raw, first_bin, F), "grp", split_axis=3, concat_axis=2, tiled=True)
    spectra = jnp.transpose(white, (3, 1, 0, 2)).reshape(
        own, seg_count, 2 * num_grp * chan_count
    )
    picks = lax.dynamic_index_in_dim(partner, lax.axis_index("blk"), 1, keepdims=False)
    chunks = 1
    while spectra.size * 2 * num_blocks // chunks > GATHER_BYTES:
        chunks *= 2

    direct = chunks == 1 and num_blocks % 4 == 0

    def one(part):
        whole = gather(part, num_blocks) if direct else lax.all_gather(part, "blk")
        return cross(part, whole, picks, 16)

    if chunks == 1:
        return one(spectra)
    result = lax.map(one, spectra.reshape(chunks, own // chunks, seg_count, -1))
    rounds = partner.shape[0]
    return jnp.moveaxis(result, 0, 1).reshape(rounds, own, *result.shape[3:])


def solution(mesh):
    placed = (P(None, ("blk", "grp"), None), P())
    return jax.shard_map(
        functools.partial(per_device, mesh.shape["blk"], mesh.shape["grp"]),
        mesh=mesh,
        in_specs=placed,
        out_specs=P(None, "grp", "blk", None),
        check_vma=False,
    )
```
